32 devices in a mesh: group: 2 (over x), lat: 16 (over z, y, core).
Axes of the slice: x: 2, y: 2, z: 4, core: 2. Of those that a mesh axis runs over, the one named last changes fastest.
Arguments:
- currents: float32 [16, 2, 512, 512], P('group', None, 'lat'), parts along dimension 0, may hold values from -6 to 6
- green: float32 [16, 8, 2, 1024, 1024], P('group', None, None, 'lat'), parts along dimension 0, may hold values from -5 to 5
- section_map: int32 [16], P('group'), parts along dimension 0, may hold values from 0 to 7
- offsets: int32 [16], P('group'), parts along dimension 0, may hold values from 0 to 512
Outputs:
- fields: float32 [16, 2, 512, 512], P('group', None, 'lat'), parts along dimension 0
The draws below stay inside these ranges and needn't reach their ends.
There are 2 independent parts, one for each index of `group`. The reference program is written for one: setup_inputs(seed, part) draws one part's arguments, and reference() takes and returns one part's arrays. A program takes and returns all parts, laid end to end along the dimension named above; each array names one. Nothing has to cross between parts.
All inputs are finite; a program needn't handle non-finite values.
Results may differ from the reference program's by a relative error of at most 0.0003.
Values sent between devices are 32-bit elements; how exact they have to be, the bound alone decides.
A program may use at most 128 MiB of HBM per device.

```python
import jax
import jax.numpy as jnp
from jax import lax

N = 512
PADDED = 1024
DEPTHS = 8
SECTIONS = 8


def place_ends(result, rng, smallest, top_value):
    spot = [jax.random.randint(jax.random.fold_in(rng, axis), (), 0, length) for axis, length in enumerate(result.shape)]
    main_axis = result.shape.index(max(result.shape))
    next_to = spot[:main_axis] + [(spot[main_axis] + 1) % result.shape[main_axis]] + spot[main_axis + 1:]
    return result.at[tuple(spot)].set(smallest).at[tuple(next_to)].set(top_value)


def steps_of(key, dims, split, low, largest):
    gain, own = 1.0, jax.random.fold_in(key, 6)
    for axis_at, parts in split:
        steps = jnp.exp(jax.random.uniform(jax.random.fold_in(own, axis_at), (parts,), jnp.float32, low / len(split), largest / len(split)))
        gain = gain * jnp.repeat(steps, dims[axis_at] // parts).reshape([-1 if axis == axis_at else 1 for axis in range(len(dims))])
    return gain


def centred(key, shape, scale, reach, split=(), kind=jnp.bfloat16):
    entries = jax.random.normal(key, shape, jnp.float32) * scale
    if len(split) > 0:
        entries = steps_of(key, shape, split, -0.22, 0.18) * entries
    return jnp.clip(entries, min=-reach, max=reach).astype(kind)


def setup_inputs(seed: int = 0, part: int = 0) -> dict:
    streams_of = jax.random.split(jax.random.key(seed), 5)
    own_keys = jax.random.split(jax.random.fold_in(streams_of[4], part), 5)
    currents = centred(own_keys[0], (DEPTHS, 2, N, N), 1.0, 6.0, ((2, 16),), jnp.float32)
    green = centred(own_keys[1], (SECTIONS, SECTIONS, 2, PADDED, PADDED), 0.35, 5.0, ((3, 16),), jnp.float32)
    section_map = place_ends(jax.random.randint(own_keys[2], (DEPTHS,), 0, SECTIONS), jax.random.fold_in(own_keys[2], 1), 0, SECTIONS - 1).astype(jnp.int32)
    offsets = place_ends(jax.random.randint(own_keys[3], (DEPTHS,), 0, N + 1), jax.random.fold_in(own_keys[3], 1), 0, N).astype(jnp.int32)
    return {"currents": currents, "green": green, "section_map": section_map, "offsets": offsets}


def embed_plane(plane, offset):
    blank = jnp.zeros((2 * N, 2 * N), plane.dtype)
    return lax.dynamic_update_slice(blank, plane, (jnp.int32(0), offset.astype(jnp.int32)))


def crop_plane(plane, offset):
    return lax.dynamic_slice(plane, (jnp.int32(0), offset.astype(jnp.int32)), (N, N))


def reference(currents, green, section_map, offsets):
    planes = lax.complex(currents[:, 0], currents[:, 1])
    spectrum = jnp.fft.fft2(jax.vmap(embed_plane)(planes, offsets))
    onehot = (section_map[:, None] == jnp.arange(SECTIONS, dtype=jnp.int32)[None, :]).astype(currents.dtype)
    section_spec = jnp.einsum("js,jab->sab", onehot.astype(spectrum.dtype), spectrum)
    green_complex = lax.complex(green[:, :, 0], green[:, :, 1])
    coupled = jnp.einsum("tsqk,skq->tkq", green_complex, section_spec)
    per_depth = jnp.einsum("js,sab->jab", onehot.astype(coupled.dtype), coupled)
    fields = jax.vmap(crop_plane)(jnp.fft.ifft2(per_depth), offsets)
    return jnp.stack([jnp.real(fields), jnp.imag(fields)], axis=1).astype(jnp.float32)
```

```python
import functools
import math

import jax
import jax.numpy as jnp
import ml_dtypes
import numpy as np
from jax import lax
from jax.experimental import pallas as pl
from jax.experimental.pallas import tpu as pltpu
from jax.sharding import PartitionSpec as P

LANES = 128
MESH = pl.DeviceIdType.MESH


def split_np(table):
    high = table.astype(ml_dtypes.bfloat16)
    low = (table - high.astype(np.float64)).astype(ml_dtypes.bfloat16)
    return np.stack([high, low])


def waves(width, period):
    angle = 2.0 * np.pi / period * (np.arange(width)[:, None] * np.arange(period)[None, :] % period)
    return np.cos(angle), np.sin(angle)


def blocked_table(width, period, block):
    cosine, sine = waves(width, period)
    parts = [cosine.reshape(width, -1, 1, block), -sine.reshape(width, -1, 1, block)]
    return np.concatenate(parts, axis=2).reshape(width, 2 * period)


def split_bf16(values):
    high = values.astype(jnp.bfloat16)
    low = (values - high.astype(jnp.float32)).astype(jnp.bfloat16)
    return high, low


def dot32(left, right):
    return jnp.dot(left, right, preferred_element_type=jnp.float32)


def dot_split(stacked, high_table, low_table):
    rows = stacked.shape[0] // 2
    both = dot32(stacked, high_table)
    return both[:rows] + both[rows:] + dot32(stacked[:rows], low_table)


def swap_halves(values):
    half = LANES // 2
    parts = []
    for start in range(0, values.shape[-1], LANES):
        parts.append(pltpu.roll(values[:, start : start + LANES], half, 1))
    return jnp.concatenate(parts, axis=1) if len(parts) > 1 else parts[0]


def section_slots(map_ref, depths, sections):
    used = []
    for section in range(sections):
        found = map_ref[0] == section
        for depth in range(1, depths):
            found = jnp.logical_or(found, map_ref[depth] == section)
        used.append(found.astype(jnp.int32))
    rank, before = [], jnp.int32(0)
    for section in range(sections):
        rank.append(before)
        before = before + used[section]
    return rank, used


def slot_of_depth(map_ref, rank, depth):
    value = jnp.int32(0)
    for section, place in enumerate(rank):
        value = jnp.where(map_ref[depth] == section, place, value)
    return value


def forward_kernel(map_ref, cur_ref, high_ref, low_ref, cos_ref, sin_ref, out_ref, split_ref):
    depths, _, rows, width = cur_ref.shape
    sections = out_ref.shape[0]
    half = depths * rows

    @pl.when(pl.program_id(0) == 0)
    def _():
        for part in range(2):
            high, low = split_bf16(cur_ref[:, part].reshape(half, width))
            split_ref[pl.ds(part * half, half), :] = high
            split_ref[pl.ds((2 + part) * half, half), :] = low

    product = dot_split(split_ref[...], high_ref[...], low_ref[...])
    lane = lax.broadcasted_iota(jnp.int32, (1, product.shape[1]), 1) % LANES
    sign = jnp.where(lane < LANES // 2, -1.0, 1.0)
    spectrum = product[:half] + swap_halves(product[half:]) * sign
    swapped = swap_halves(spectrum)
    rank, _ = section_slots(map_ref, depths, sections)
    out_ref[...] = jnp.zeros_like(out_ref)
    for depth in range(depths):
        span = slice(depth * rows, (depth + 1) * rows)
        turned = (
            spectrum[span] * cos_ref[pl.ds(depth, 1), :]
            + swapped[span] * sin_ref[pl.ds(depth, 1), :]
        )
        out_ref[slot_of_depth(map_ref, rank, depth)] += turned


def inverse_kernel(map_ref, ret_ref, high_ref, low_ref, cos_ref, sin_ref, out_ref, split_ref):
    depths, _, rows, width = out_ref.shape
    sections = ret_ref.shape[0]
    half = depths * rows
    lanes = ret_ref.shape[2]

    @pl.when(pl.program_id(0) == 0)
    def _():
        rank, _ = section_slots(map_ref, depths, sections)
        lane = lax.broadcasted_iota(jnp.int32, (1, lanes), 1) % LANES
        sign = jnp.where(lane < LANES // 2, 1.0, -1.0)
        for depth in range(depths):
            plane = ret_ref[slot_of_depth(map_ref, rank, depth)]
            turned = (
                plane * cos_ref[pl.ds(depth, 1), :]
                - swap_halves(plane) * sin_ref[pl.ds(depth, 1), :]
            )
            crossed = swap_halves(turned) * sign
            for part, values in enumerate((turned, crossed)):
                high, low = split_bf16(values)
                split_ref[pl.ds(part * half + depth * rows, rows), :] = high
                split_ref[pl.ds((2 + part) * half + depth * rows, rows), :] = low

    product = dot_split(split_ref[...], high_ref[...], low_ref[...])
    scale = 4.0 / (lanes * lanes)
    for part in range(2):
        out_ref[:, part] = (product[part * half : (part + 1) * half] * scale).reshape(
            depths, rows, width
        )


def exchange_kernel(
    n, slots, map_ref, src_ref, green_hbm, table_hbm, back_hbm, out_ref,
    recv, green, table, back, spectra, total, result,
    send_sem, recv_sem, send_back, recv_back, load_sem, green_sem,
):
    group = lax.axis_index("group")
    me = lax.axis_index("lat")
    rows = src_ref.shape[1]
    sections, block, period = green.shape[0], green.shape[3], green.shape[4]
    width = recv.shape[1]
    tables_in = pltpu.make_async_copy(table_hbm, table, load_sem.at[0])
    back_in = pltpu.make_async_copy(back_hbm, back, load_sem.at[1])
    green_in = pltpu.make_async_copy(green_hbm, green, green_sem)
    tables_in.start()

    barrier = pltpu.get_barrier_semaphore()

    def greet(step, carry):
        other = lax.rem(me + step, n)
        pl.semaphore_signal(barrier, inc=1, device_id=(group, other), device_id_type=MESH)
        return carry

    lax.fori_loop(1, n, greet, 0)
    pl.semaphore_wait(barrier, n - 1)

    my_rows = pl.ds(pl.multiple_of(me * rows, rows), rows)
    my_lanes = pl.ds(pl.multiple_of(me * LANES, LANES), LANES)

    def send_sources(base, count):
        batch = pl.ds(base, count)
        pltpu.make_async_copy(
            src_ref.at[batch, :, my_lanes], recv.at[batch, my_rows], recv_sem.at[base // 2]
        ).start()

        def send(step, carry):
            other = lax.rem(me + step, n)
            pltpu.make_async_remote_copy(
                src_ref=src_ref.at[batch, :, pl.ds(pl.multiple_of(other * LANES, LANES), LANES)],
                dst_ref=recv.at[batch, my_rows],
                send_sem=send_sem,
                recv_sem=recv_sem.at[base // 2],
                device_id=(group, other),
                device_id_type=MESH,
            ).start()
            return carry

        lax.fori_loop(1, n, send, 0)

    def send_results(base, count):
        batch = pl.ds(base, count)
        pltpu.make_async_copy(
            result.at[batch, my_rows], out_ref.at[batch, :, my_lanes], recv_back
        ).start()

        def send(step, carry):
            other = lax.rem(me + step, n)
            pltpu.make_async_remote_copy(
                src_ref=result.at[batch, pl.ds(pl.multiple_of(other * rows, rows), rows)],
                dst_ref=out_ref.at[batch, :, my_lanes],
                send_sem=send_back,
                recv_sem=recv_back,
                device_id=(group, other),
                device_id_type=MESH,
            ).start()
            return carry

        lax.fori_loop(1, n, send, 0)

    def batches(body):
        def pair(index, carry):
            body(index * 2, 2)
            return carry

        lax.fori_loop(0, slots // 2, pair, 0)
        if slots % 2:
            body(slots - 1, 1)

    batches(send_sources)
    green_in.start()
    back_in.start()

    rank, used = section_slots(map_ref, map_ref.shape[0], sections)
    place = []
    for slot in range(slots):
        found = jnp.int32(0)
        for section in range(sections):
            here = jnp.logical_and(rank[section] == slot, used[section] == 1)
            found = jnp.where(here, section, found)
        place.append(found)

    def place_of(slot):
        found = place[0]
        for index in range(1, slots):
            found = jnp.where(slot == index, place[index], found)
        return found

    total[...] = jnp.zeros_like(total)
    tables_in.wait()
    chunk = 2 * LANES

    def take(base, count):
        arrived = recv.at[pl.ds(base, count)]
        pltpu.make_async_copy(arrived, arrived, recv_sem.at[base // 2]).wait()
        halves = [jnp.transpose(recv[base + index]) for index in range(count)]
        stacked = jnp.concatenate(halves, axis=0) if count > 1 else halves[0]
        high, low = split_bf16(stacked)
        stacked = jnp.concatenate([high, low], axis=0)

        def columns(index, carry):
            span = pl.ds(pl.multiple_of(index * chunk, chunk), chunk)
            by_cos = dot_split(stacked, table[0, 0, :, span], table[0, 1, :, span])
            by_sin = dot_split(stacked, table[1, 0, :, span], table[1, 1, :, span])
            for slot in range(count):
                real = slice(slot * 2 * block, slot * 2 * block + block)
                imag = slice(slot * 2 * block + block, (slot + 1) * 2 * block)
                spectra[slot, 0, :, span] = by_cos[real] + by_sin[imag]
                spectra[slot, 1, :, span] = by_cos[imag] - by_sin[real]
            return carry

        lax.fori_loop(0, period // chunk, columns, 0)

        @pl.when(base == 0)
        def _():
            green_in.wait()

        froms = [place_of(base + index) for index in range(count)]

        def couple(index, carry):
            span = pl.ds(pl.multiple_of(index * 8, 8), 8)
            source = [(spectra[i, 0, span, :], spectra[i, 1, span, :]) for i in range(count)]
            for slot in range(slots):
                real = total[slot, 0, span, :]
                imag = total[slot, 1, span, :]
                for i in range(count):
                    green_real = green[place[slot], froms[i], 0, span, :]
                    green_imag = green[place[slot], froms[i], 1, span, :]
                    real = real + green_real * source[i][0] - green_imag * source[i][1]
                    imag = imag + green_real * source[i][1] + green_imag * source[i][0]
                total[slot, 0, span, :] = real
                total[slot, 1, span, :] = imag
            return carry

        lax.fori_loop(0, block // 8, couple, 0)

    batches(take)
    back_in.wait()

    def give(base, count):
        stacked = total[pl.ds(base, count)].reshape(count * 2 * block, period)
        high, low = split_bf16(stacked)
        stacked = jnp.concatenate([high, low], axis=0)

        def columns(index, carry):
            span = pl.ds(pl.multiple_of(index * chunk, chunk), chunk)
            by_cos = dot_split(stacked, back[0, 0, :, span], back[0, 1, :, span])
            by_sin = dot_split(stacked, back[1, 0, :, span], back[1, 1, :, span])
            for slot in range(count):
                real = slice(slot * 2 * block, slot * 2 * block + block)
                imag = slice(slot * 2 * block + block, (slot + 1) * 2 * block)
                plane = jnp.concatenate(
                    [by_cos[real] - by_sin[imag], by_cos[imag] + by_sin[real]], axis=0
                )
                result[base + slot, span, :] = jnp.transpose(plane)
            return carry

        lax.fori_loop(0, width // chunk, columns, 0)
        send_results(base, count)

    batches(give)
    landed = out_ref.at[pl.ds(0, slots)]
    pltpu.make_async_copy(landed, landed, recv_back).wait()
    left = src_ref.at[pl.ds(0, slots), :, pl.ds(LANES, (n - 1) * LANES)]
    pltpu.make_async_copy(left, left, send_sem).wait()
    gone = result.at[pl.ds(0, slots), pl.ds(rows, width - rows)]
    pltpu.make_async_copy(gone, gone, send_back).wait()


def per_device_kernels(n, currents, green, section_map, offsets):
    depths, _, rows, width = currents.shape
    sections, _, _, block, period = green.shape
    lanes = 2 * period
    f32, bf16 = jnp.float32, jnp.bfloat16
    cosine, sine = waves(width, period)
    blocked = blocked_table(width, period, block)
    spread = jnp.asarray(split_np(blocked))
    gather = jnp.asarray(split_np(np.ascontiguousarray(blocked.T)))
    table = jnp.asarray(np.stack([split_np(cosine), split_np(sine)]))
    back = jnp.asarray(np.stack([split_np(np.ascontiguousarray(cosine.T)),
                                 split_np(np.ascontiguousarray(sine.T))]))
    lane = lax.iota(jnp.int32, lanes)
    wavenumber = lane // (2 * block) * block + lane % block
    angles = 2.0 * math.pi / period * (offsets[:, None] * wavenumber[None, :] % period).astype(f32)
    turn_cos = jnp.cos(angles)
    turn_sin = jnp.sin(angles) * jnp.where(lane % (2 * block) < block, 1.0, -1.0)
    limit = 60 * 2**20
    smem = pl.BlockSpec(memory_space=pltpu.SMEM)
    anywhere = pl.BlockSpec(memory_space=pl.ANY)
    column = 2 * LANES
    sources = pl.pallas_call(
        forward_kernel,
        grid=(lanes // column,),
        out_shape=jax.ShapeDtypeStruct((sections, rows, lanes), f32),
        in_specs=[
            smem,
            pl.BlockSpec((depths, 2, rows, width), lambda i: (0, 0, 0, 0)),
            pl.BlockSpec((None, width, column), lambda i: (0, 0, i)),
            pl.BlockSpec((None, width, column), lambda i: (1, 0, i)),
            pl.BlockSpec((depths, column), lambda i: (0, i)),
            pl.BlockSpec((depths, column), lambda i: (0, i)),
        ],
        out_specs=pl.BlockSpec((sections, rows, column), lambda i: (0, 0, i)),
        scratch_shapes=[pltpu.VMEM((4 * depths * rows, width), bf16)],
        compiler_params=pltpu.CompilerParams(vmem_limit_bytes=32 * 2**20),
    )(section_map, currents, spread, spread, turn_cos, turn_sin)

    def exchange(slots):
        return pl.pallas_call(
            functools.partial(exchange_kernel, n, slots),
            out_shape=jax.ShapeDtypeStruct((sections, rows, lanes), f32),
            in_specs=[smem] + [anywhere] * 4,
            out_specs=anywhere,
            scratch_shapes=[
                pltpu.VMEM((slots, width, LANES), f32),
                pltpu.VMEM(green.shape, f32),
                pltpu.VMEM(table.shape, bf16),
                pltpu.VMEM(back.shape, bf16),
                pltpu.VMEM((2, 2, block, period), f32),
                pltpu.VMEM((slots, 2, block, period), f32),
                pltpu.VMEM((slots, width, LANES), f32),
                pltpu.SemaphoreType.DMA,
                pltpu.SemaphoreType.DMA(((slots + 1) // 2,)),
                pltpu.SemaphoreType.DMA,
                pltpu.SemaphoreType.DMA,
                pltpu.SemaphoreType.DMA((2,)),
                pltpu.SemaphoreType.DMA,
            ],
            compiler_params=pltpu.CompilerParams(
                collective_id=slots, has_side_effects=True, vmem_limit_bytes=limit
            ),
        )

    returned = exchange(sections)(section_map, sources, green, table, back)
    return pl.pallas_call(
        inverse_kernel,
        grid=(width // column,),
        out_shape=jax.ShapeDtypeStruct(currents.shape, f32),
        in_specs=[
            smem,
            pl.BlockSpec((sections, rows, lanes), lambda i: (0, 0, 0)),
            pl.BlockSpec((None, lanes, column), lambda i: (0, 0, i)),
            pl.BlockSpec((None, lanes, column), lambda i: (1, 0, i)),
            pl.BlockSpec((depths, lanes), lambda i: (0, 0)),
            pl.BlockSpec((depths, lanes), lambda i: (0, 0)),
        ],
        out_specs=pl.BlockSpec((depths, 2, rows, column), lambda i: (0, 0, 0, i)),
        scratch_shapes=[pltpu.VMEM((4 * depths * rows, lanes), bf16)],
        compiler_params=pltpu.CompilerParams(vmem_limit_bytes=40 * 2**20),
    )(section_map, returned, gather, gather, turn_cos, turn_sin)


def dft_table(n_in, n_out, period, sign_value):
    row_ids = lax.iota(jnp.int32, n_in)
    col_ids = lax.iota(jnp.int32, n_out)
    angles = (
        2.0 * math.pi / period * (row_ids[:, None] * col_ids[None, :] % period).astype(jnp.float32)
    )
    cosine = jnp.cos(angles)
    sine_part = sign_value * jnp.sin(angles)
    return jnp.stack(
        [jnp.stack([cosine, sine_part], axis=1), jnp.stack([-sine_part, cosine], axis=1)], axis=0
    )


def phases(offsets, period, sign_value):
    col_ids = lax.iota(jnp.int32, period)
    angles = (
        2.0 * math.pi / period * (offsets[:, None] * col_ids[None, :] % period).astype(jnp.float32)
    )
    return (jnp.cos(angles)[:, None, :], sign_value * jnp.sin(angles)[:, None, :])


def rotate(planes, cosine, sine_part):
    real_part = planes[:, 0] * cosine - planes[:, 1] * sine_part
    imag_part = planes[:, 0] * sine_part + planes[:, 1] * cosine
    return jnp.stack([real_part, imag_part], axis=1)


def per_device(currents, green, section_map, offsets):
    highest = lax.Precision.HIGHEST
    plane_width = currents.shape[3]
    padded = 2 * plane_width
    sections = green.shape[0]
    forward = dft_table(plane_width, padded, padded, -1.0)
    inverse = dft_table(padded, plane_width, padded, 1.0)
    onehot = (section_map[:, None] == lax.iota(jnp.int32, sections)[None, :]).astype(jnp.float32)
    spec_y = jnp.einsum("jcxy,cydk->jdxk", currents, forward, precision=highest)
    cos_fwd, sin_fwd = phases(offsets, padded, -1.0)
    shifted = jnp.transpose(rotate(spec_y, cos_fwd, sin_fwd), (0, 2, 1, 3))
    grouped = jnp.einsum("js,jxdk->sxdk", onehot, shifted, precision=highest)
    spectra = jnp.einsum(
        "mxcq,cxdk->mdqk",
        lax.all_to_all(grouped, "lat", split_axis=3, concat_axis=1, tiled=True),
        forward,
        precision=highest,
    )
    green_real = green[:, :, 0]
    green_imag = green[:, :, 1]
    out_real = jnp.einsum(
        "tsqk,sqk->tqk", green_real, spectra[:, 0], precision=highest
    ) - jnp.einsum("tsqk,sqk->tqk", green_imag, spectra[:, 1], precision=highest)
    out_imag = jnp.einsum(
        "tsqk,sqk->tqk", green_real, spectra[:, 1], precision=highest
    ) + jnp.einsum("tsqk,sqk->tqk", green_imag, spectra[:, 0], precision=highest)
    coupled = jnp.stack([out_real, out_imag], axis=1)
    returned = lax.all_to_all(
        jnp.einsum("mcqk,ckdx->mdxq", coupled, inverse, precision=highest),
        "lat",
        split_axis=2,
        concat_axis=3,
        tiled=True,
    )
    per_depth = jnp.einsum("js,sdxq->jdxq", onehot, returned, precision=highest)
    cos_back, sin_back = phases(offsets, padded, 1.0)
    turned = rotate(per_depth, cos_back, sin_back)
    result = jnp.einsum("jcxk,ckdy->jdxy", turned, inverse, precision=highest)
    return result * (1.0 / (padded * padded))


def solution(mesh):
    in_specs = (
        P("group", None, "lat", None),
        P("group", None, None, "lat", None),
        P("group"),
        P("group"),
    )
    out_specs = P("group", None, "lat", None)
    n = mesh.shape["lat"]

    def either(currents, green, section_map, offsets):
        fits = 2 * green.shape[3] == LANES and currents.shape[2] % 16 == 0
        if fits and currents.shape[3] % (2 * LANES) == 0:
            return per_device_kernels(n, currents, green, section_map, offsets)
        return per_device(currents, green, section_map, offsets)

    return jax.shard_map(
        either, mesh=mesh, in_specs=in_specs, out_specs=out_specs, check_vma=False
    )
```

```python
import functools
import math

import jax
import jax.numpy as jnp
import ml_dtypes
import numpy as np
from jax import lax
from jax.experimental import pallas as pl
from jax.experimental.pallas import tpu as pltpu
from jax.sharding import PartitionSpec as P

LANES = 128
MESH = pl.DeviceIdType.MESH


def split_np(table):
    high = table.astype(ml_dtypes.bfloat16)
    low = (table - high.astype(np.float64)).astype(ml_dtypes.bfloat16)
    return np.stack([high, low])


def waves(width, period):
    angle = 2.0 * np.pi / period * (np.arange(width)[:, None] * np.arange(period)[None, :] % period)
    return np.cos(angle), np.sin(angle)


def blocked_table(width, period, block):
    cosine, sine = waves(width, period)
    parts = [cosine.reshape(width, -1, 1, block), -sine.reshape(width, -1, 1, block)]
    return np.concatenate(parts, axis=2).reshape(width, 2 * period)


def split_bf16(values):
    high = values.astype(jnp.bfloat16)
    low = (values - high.astype(jnp.float32)).astype(jnp.bfloat16)
    return high, low


def dot32(left, right):
    return jnp.dot(left, right, preferred_element_type=jnp.float32)


def dot_split(stacked, high_table, low_table):
    rows = stacked.shape[0] // 2
    both = dot32(stacked, high_table)
    return both[:rows] + both[rows:] + dot32(stacked[:rows], low_table)


def swap_halves(values):
    half = LANES // 2
    parts = []
    for start in range(0, values.shape[-1], LANES):
        parts.append(pltpu.roll(values[:, start : start + LANES], half, 1))
    return jnp.concatenate(parts, axis=1) if len(parts) > 1 else parts[0]


def section_slots(map_ref, depths, sections):
    used = []
    for section in range(sections):
        found = map_ref[0] == section
        for depth in range(1, depths):
            found = jnp.logical_or(found, map_ref[depth] == section)
        used.append(found.astype(jnp.int32))
    rank, before = [], jnp.int32(0)
    for section in range(sections):
        rank.append(before)
        before = before + used[section]
    return rank, used


def slot_of_depth(map_ref, rank, depth):
    value = jnp.int32(0)
    for section, place in enumerate(rank):
        value = jnp.where(map_ref[depth] == section, place, value)
    return value


def forward_kernel(map_ref, cur_ref, high_ref, low_ref, cos_ref, sin_ref, out_ref, split_ref):
    depths, _, rows, width = cur_ref.shape
    sections = out_ref.shape[0]
    half = depths * rows

    @pl.when(pl.program_id(0) == 0)
    def _():
        for part in range(2):
            high, low = split_bf16(cur_ref[:, part].reshape(half, width))
            split_ref[pl.ds(part * half, half), :] = high
            split_ref[pl.ds((2 + part) * half, half), :] = low

    product = dot_split(split_ref[...], high_ref[...], low_ref[...])
    lane = lax.broadcasted_iota(jnp.int32, (1, product.shape[1]), 1) % LANES
    sign = jnp.where(lane < LANES // 2, -1.0, 1.0)
    spectrum = product[:half] + swap_halves(product[half:]) * sign
    swapped = swap_halves(spectrum)
    rank, _ = section_slots(map_ref, depths, sections)
    out_ref[...] = jnp.zeros_like(out_ref)
    for depth in range(depths):
        span = slice(depth * rows, (depth + 1) * rows)
        turned = (
            spectrum[span] * cos_ref[pl.ds(depth, 1), :]
            + swapped[span] * sin_ref[pl.ds(depth, 1), :]
        )
        out_ref[slot_of_depth(map_ref, rank, depth)] += turned


def inverse_kernel(map_ref, ret_ref, high_ref, low_ref, cos_ref, sin_ref, out_ref, split_ref):
    depths, _, rows, width = out_ref.shape
    sections = ret_ref.shape[0]
    half = depths * rows
    lanes = ret_ref.shape[2]

    @pl.when(pl.program_id(0) == 0)
    def _():
        rank, _ = section_slots(map_ref, depths, sections)
        lane = lax.broadcasted_iota(jnp.int32, (1, lanes), 1) % LANES
        sign = jnp.where(lane < LANES // 2, 1.0, -1.0)
        for depth in range(depths):
            plane = ret_ref[slot_of_depth(map_ref, rank, depth)]
            turned = (
                plane * cos_ref[pl.ds(depth, 1), :]
                - swap_halves(plane) * sin_ref[pl.ds(depth, 1), :]
            )
            crossed = swap_halves(turned) * sign
            for part, values in enumerate((turned, crossed)):
                high, low = split_bf16(values)
                split_ref[pl.ds(part * half + depth * rows, rows), :] = high
                split_ref[pl.ds((2 + part) * half + depth * rows, rows), :] = low

    product = dot_split(split_ref[...], high_ref[...], low_ref[...])
    scale = 4.0 / (lanes * lanes)
    for part in range(2):
        out_ref[:, part] = (product[part * half : (part + 1) * half] * scale).reshape(
            depths, rows, width
        )


def exchange_kernel(
    n, slots, map_ref, src_ref, green_hbm, table_hbm, back_hbm, out_ref,
    recv, green, table, back, spectra, total, result,
    send_sem, recv_sem, send_back, recv_back, load_sem, green_sem,
):
    group = lax.axis_index("group")
    me = lax.axis_index("lat")
    rows = src_ref.shape[1]
    sections, block, period = green.shape[0], green.shape[3], green.shape[4]
    width = recv.shape[1]
    tables_in = pltpu.make_async_copy(table_hbm, table, load_sem.at[0])
    back_in = pltpu.make_async_copy(back_hbm, back, load_sem.at[1])
    green_in = pltpu.make_async_copy(green_hbm, green, green_sem)
    tables_in.start()

    barrier = pltpu.get_barrier_semaphore()

    def greet(step, carry):
        other = lax.rem(me + step, n)
        pl.semaphore_signal(barrier, inc=1, device_id=(group, other), device_id_type=MESH)
        return carry

    lax.fori_loop(1, n, greet, 0)
    pl.semaphore_wait(barrier, n - 1)

    my_rows = pl.ds(pl.multiple_of(me * rows, rows), rows)
    my_lanes = pl.ds(pl.multiple_of(me * LANES, LANES), LANES)

    def send_sources(base, count):
        batch = pl.ds(base, count)
        pltpu.make_async_copy(
            src_ref.at[batch, :, my_lanes], recv.at[batch, my_rows], recv_sem.at[base // 2]
        ).start()

        def send(step, carry):
            other = lax.rem(me + step, n)
            pltpu.make_async_remote_copy(
                src_ref=src_ref.at[batch, :, pl.ds(pl.multiple_of(other * LANES, LANES), LANES)],
                dst_ref=recv.at[batch, my_rows],
                send_sem=send_sem,
                recv_sem=recv_sem.at[base // 2],
                device_id=(group, other),
                device_id_type=MESH,
            ).start()
            return carry

        lax.fori_loop(1, n, send, 0)

    def send_results(base, count):
        batch = pl.ds(base, count)
        pltpu.make_async_copy(
            result.at[batch, my_rows], out_ref.at[batch, :, my_lanes], recv_back
        ).start()

        def send(step, carry):
            other = lax.rem(me + step, n)
            pltpu.make_async_remote_copy(
                src_ref=result.at[batch, pl.ds(pl.multiple_of(other * rows, rows), rows)],
                dst_ref=out_ref.at[batch, :, my_lanes],
                send_sem=send_back,
                recv_sem=recv_back,
                device_id=(group, other),
                device_id_type=MESH,
            ).start()
            return carry

        lax.fori_loop(1, n, send, 0)

    def batches(body):
        def pair(index, carry):
            body(index * 2, 2)
            return carry

        lax.fori_loop(0, slots // 2, pair, 0)
        if slots % 2:
            body(slots - 1, 1)

    batches(send_sources)
    green_in.start()
    back_in.start()

    rank, used = section_slots(map_ref, map_ref.shape[0], sections)
    place = []
    for slot in range(slots):
        found = jnp.int32(0)
        for section in range(sections):
            here = jnp.logical_and(rank[section] == slot, used[section] == 1)
            found = jnp.where(here, section, found)
        place.append(found)

    def place_of(slot):
        found = place[0]
        for index in range(1, slots):
            found = jnp.where(slot == index, place[index], found)
        return found

    total[...] = jnp.zeros_like(total)
    tables_in.wait()
    chunk = 2 * LANES

    def take(base, count):
        arrived = recv.at[pl.ds(base, count)]
        pltpu.make_async_copy(arrived, arrived, recv_sem.at[base // 2]).wait()
        halves = [jnp.transpose(recv[base + index]) for index in range(count)]
        stacked = jnp.concatenate(halves, axis=0) if count > 1 else halves[0]
        high, low = split_bf16(stacked)
        stacked = jnp.concatenate([high, low], axis=0)

        def columns(index, carry):
            span = pl.ds(pl.multiple_of(index * chunk, chunk), chunk)
            by_cos = dot_split(stacked, table[0, 0, :, span], table[0, 1, :, span])
            by_sin = dot_split(stacked, table[1, 0, :, span], table[1, 1, :, span])
            for slot in range(count):
                real = slice(slot * 2 * block, slot * 2 * block + block)
                imag = slice(slot * 2 * block + block, (slot + 1) * 2 * block)
                spectra[slot, 0, :, span] = by_cos[real] + by_sin[imag]
                spectra[slot, 1, :, span] = by_cos[imag] - by_sin[real]
            return carry

        lax.fori_loop(0, period // chunk, columns, 0)

        @pl.when(base == 0)
        def _():
            green_in.wait()

        froms = [place_of(base + index) for index in range(count)]

        def couple(index, carry):
            span = pl.ds(pl.multiple_of(index * 8, 8), 8)
            source = [(spectra[i, 0, span, :], spectra[i, 1, span, :]) for i in range(count)]
            for slot in range(slots):
                real = total[slot, 0, span, :]
                imag = total[slot, 1, span, :]
                for i in range(count):
                    green_real = green[place[slot], froms[i], 0, span, :]
                    green_imag = green[place[slot], froms[i], 1, span, :]
                    real = real + green_real * source[i][0] - green_imag * source[i][1]
                    imag = imag + green_real * source[i][1] + green_imag * source[i][0]
                total[slot, 0, span, :] = real
                total[slot, 1, span, :] = imag
            return carry

        lax.fori_loop(0, block // 8, couple, 0)

    batches(take)
    back_in.wait()

    def give(base, count):
        stacked = total[pl.ds(base, count)].reshape(count * 2 * block, period)
        high, low = split_bf16(stacked)
        stacked = jnp.concatenate([high, low], axis=0)

        def columns(index, carry):
            span = pl.ds(pl.multiple_of(index * chunk, chunk), chunk)
            by_cos = dot_split(stacked, back[0, 0, :, span], back[0, 1, :, span])
            by_sin = dot_split(stacked, back[1, 0, :, span], back[1, 1, :, span])
            for slot in range(count):
                real = slice(slot * 2 * block, slot * 2 * block + block)
                imag = slice(slot * 2 * block + block, (slot + 1) * 2 * block)
                plane = jnp.concatenate(
                    [by_cos[real] - by_sin[imag], by_cos[imag] + by_sin[real]], axis=0
                )
                result[base + slot, span, :] = jnp.transpose(plane)
            return carry

        lax.fori_loop(0, width // chunk, columns, 0)
        send_results(base, count)

    batches(give)
    landed = out_ref.at[pl.ds(0, slots)]
    pltpu.make_async_copy(landed, landed, recv_back).wait()
    left = src_ref.at[pl.ds(0, slots), :, pl.ds(LANES, (n - 1) * LANES)]
    pltpu.make_async_copy(left, left, send_sem).wait()
    gone = result.at[pl.ds(0, slots), pl.ds(rows, width - rows)]
    pltpu.make_async_copy(gone, gone, send_back).wait()


def most_sections(section_map, groups):
    bits = lax.reduce(
        jnp.left_shift(jnp.int32(1), section_map), np.int32(0), lax.bitwise_or, (0,)
    )
    count = lax.population_count(bits)
    most = count
    for shift in range(1, groups):
        ring = [(group, (group + shift) % groups) for group in range(groups)]
        most = jnp.maximum(most, lax.ppermute(count, "group", ring))
    return most


def per_device_kernels(n, groups, currents, green, section_map, offsets):
    depths, _, rows, width = currents.shape
    sections, _, _, block, period = green.shape
    lanes = 2 * period
    most = most_sections(section_map, groups)
    f32, bf16 = jnp.float32, jnp.bfloat16
    cosine, sine = waves(width, period)
    blocked = blocked_table(width, period, block)
    spread = jnp.asarray(split_np(blocked))
    gather = jnp.asarray(split_np(np.ascontiguousarray(blocked.T)))
    table = jnp.asarray(np.stack([split_np(cosine), split_np(sine)]))
    back = jnp.asarray(np.stack([split_np(np.ascontiguousarray(cosine.T)),
                                 split_np(np.ascontiguousarray(sine.T))]))
    lane = lax.iota(jnp.int32, lanes)
    wavenumber = lane // (2 * block) * block + lane % block
    angles = 2.0 * math.pi / period * (offsets[:, None] * wavenumber[None, :] % period).astype(f32)
    turn_cos = jnp.cos(angles)
    turn_sin = jnp.sin(angles) * jnp.where(lane % (2 * block) < block, 1.0, -1.0)
    limit = 60 * 2**20
    smem = pl.BlockSpec(memory_space=pltpu.SMEM)
    anywhere = pl.BlockSpec(memory_space=pl.ANY)
    column = 2 * LANES
    sources = pl.pallas_call(
        forward_kernel,
        grid=(lanes // column,),
        out_shape=jax.ShapeDtypeStruct((sections, rows, lanes), f32),
        in_specs=[
            smem,
            pl.BlockSpec((depths, 2, rows, width), lambda i: (0, 0, 0, 0)),
            pl.BlockSpec((None, width, column), lambda i: (0, 0, i)),
            pl.BlockSpec((None, width, column), lambda i: (1, 0, i)),
            pl.BlockSpec((depths, column), lambda i: (0, i)),
            pl.BlockSpec((depths, column), lambda i: (0, i)),
        ],
        out_specs=pl.BlockSpec((sections, rows, column), lambda i: (0, 0, i)),
        scratch_shapes=[pltpu.VMEM((4 * depths * rows, width), bf16)],
        cost_estimate=pl.CostEstimate(
            flops=12 * depths * rows * width * lanes, bytes_accessed=7 * 2**20, transcendentals=0
        ),
        compiler_params=pltpu.CompilerParams(vmem_limit_bytes=limit),
    )(section_map, currents, spread, spread, turn_cos, turn_sin)

    def exchange(slots):
        return pl.pallas_call(
            functools.partial(exchange_kernel, n, slots),
            out_shape=jax.ShapeDtypeStruct((sections, rows, lanes), f32),
            in_specs=[smem] + [anywhere] * 4,
            out_specs=anywhere,
            scratch_shapes=[
                pltpu.VMEM((slots, width, LANES), f32),
                pltpu.VMEM(green.shape, f32),
                pltpu.VMEM(table.shape, bf16),
                pltpu.VMEM(back.shape, bf16),
                pltpu.VMEM((2, 2, block, period), f32),
                pltpu.VMEM((slots, 2, block, period), f32),
                pltpu.VMEM((slots, width, LANES), f32),
                pltpu.SemaphoreType.DMA,
                pltpu.SemaphoreType.DMA(((slots + 1) // 2,)),
                pltpu.SemaphoreType.DMA,
                pltpu.SemaphoreType.DMA,
                pltpu.SemaphoreType.DMA((2,)),
                pltpu.SemaphoreType.DMA,
            ],
            compiler_params=pltpu.CompilerParams(
                collective_id=slots, has_side_effects=True, vmem_limit_bytes=limit
            ),
        )

    fewest = sections // 2 + 1
    branches = [exchange(slots) for slots in range(fewest, sections + 1)]
    branch = jnp.clip(most - fewest, 0, sections - fewest)
    returned = lax.switch(branch, branches, section_map, sources, green, table, back)
    return pl.pallas_call(
        inverse_kernel,
        grid=(width // column,),
        out_shape=jax.ShapeDtypeStruct(currents.shape, f32),
        in_specs=[
            smem,
            pl.BlockSpec((sections, rows, lanes), lambda i: (0, 0, 0)),
            pl.BlockSpec((None, lanes, column), lambda i: (0, 0, i)),
            pl.BlockSpec((None, lanes, column), lambda i: (1, 0, i)),
            pl.BlockSpec((depths, lanes), lambda i: (0, 0)),
            pl.BlockSpec((depths, lanes), lambda i: (0, 0)),
        ],
        out_specs=pl.BlockSpec((depths, 2, rows, column), lambda i: (0, 0, 0, i)),
        scratch_shapes=[pltpu.VMEM((4 * depths * rows, lanes), bf16)],
        compiler_params=pltpu.CompilerParams(vmem_limit_bytes=limit),
    )(section_map, returned, gather, gather, turn_cos, turn_sin)


def dft_table(n_in, n_out, period, sign_value):
    row_ids = lax.iota(jnp.int32, n_in)
    col_ids = lax.iota(jnp.int32, n_out)
    angles = (
        2.0 * math.pi / period * (row_ids[:, None] * col_ids[None, :] % period).astype(jnp.float32)
    )
    cosine = jnp.cos(angles)
    sine_part = sign_value * jnp.sin(angles)
    return jnp.stack(
        [jnp.stack([cosine, sine_part], axis=1), jnp.stack([-sine_part, cosine], axis=1)], axis=0
    )


def phases(offsets, period, sign_value):
    col_ids = lax.iota(jnp.int32, period)
    angles = (
        2.0 * math.pi / period * (offsets[:, None] * col_ids[None, :] % period).astype(jnp.float32)
    )
    return (jnp.cos(angles)[:, None, :], sign_value * jnp.sin(angles)[:, None, :])


def rotate(planes, cosine, sine_part):
    real_part = planes[:, 0] * cosine - planes[:, 1] * sine_part
    imag_part = planes[:, 0] * sine_part + planes[:, 1] * cosine
    return jnp.stack([real_part, imag_part], axis=1)


def per_device(currents, green, section_map, offsets):
    highest = lax.Precision.HIGHEST
    plane_width = currents.shape[3]
    padded = 2 * plane_width
    sections = green.shape[0]
    forward = dft_table(plane_width, padded, padded, -1.0)
    inverse = dft_table(padded, plane_width, padded, 1.0)
    onehot = (section_map[:, None] == lax.iota(jnp.int32, sections)[None, :]).astype(jnp.float32)
    spec_y = jnp.einsum("jcxy,cydk->jdxk", currents, forward, precision=highest)
    cos_fwd, sin_fwd = phases(offsets, padded, -1.0)
    shifted = jnp.transpose(rotate(spec_y, cos_fwd, sin_fwd), (0, 2, 1, 3))
    grouped = jnp.einsum("js,jxdk->sxdk", onehot, shifted, precision=highest)
    spectra = jnp.einsum(
        "mxcq,cxdk->mdqk",
        lax.all_to_all(grouped, "lat", split_axis=3, concat_axis=1, tiled=True),
        forward,
        precision=highest,
    )
    green_real = green[:, :, 0]
    green_imag = green[:, :, 1]
    out_real = jnp.einsum(
        "tsqk,sqk->tqk", green_real, spectra[:, 0], precision=highest
    ) - jnp.einsum("tsqk,sqk->tqk", green_imag, spectra[:, 1], precision=highest)
    out_imag = jnp.einsum(
        "tsqk,sqk->tqk", green_real, spectra[:, 1], precision=highest
    ) + jnp.einsum("tsqk,sqk->tqk", green_imag, spectra[:, 0], precision=highest)
    coupled = jnp.stack([out_real, out_imag], axis=1)
    returned = lax.all_to_all(
        jnp.einsum("mcqk,ckdx->mdxq", coupled, inverse, precision=highest),
        "lat",
        split_axis=2,
        concat_axis=3,
        tiled=True,
    )
    per_depth = jnp.einsum("js,sdxq->jdxq", onehot, returned, precision=highest)
    cos_back, sin_back = phases(offsets, padded, 1.0)
    turned = rotate(per_depth, cos_back, sin_back)
    result = jnp.einsum("jcxk,ckdy->jdxy", turned, inverse, precision=highest)
    return result * (1.0 / (padded * padded))


def solution(mesh):
    in_specs = (
        P("group", None, "lat", None),
        P("group", None, None, "lat", None),
        P("group"),
        P("group"),
    )
    out_specs = P("group", None, "lat", None)
    n, groups = mesh.shape["lat"], mesh.shape["group"]

    def either(currents, green, section_map, offsets):
        fits = 2 * green.shape[3] == LANES and green.shape[0] < 32 and currents.shape[2] % 16 == 0
        if fits and currents.shape[3] % (2 * LANES) == 0:
            return per_device_kernels(n, groups, currents, green, section_map, offsets)
        return per_device(currents, green, section_map, offsets)

    return jax.shard_map(
        either, mesh=mesh, in_specs=in_specs, out_specs=out_specs, check_vma=False
    )
```

```python
import functools
import math

import jax
import jax.numpy as jnp
import ml_dtypes
import numpy as np
from jax import lax
from jax.experimental import pallas as pl
from jax.experimental.pallas import tpu as pltpu
from jax.sharding import PartitionSpec as P

LANES = 128
MESH = pl.DeviceIdType.MESH


def split_np(table):
    high = table.astype(ml_dtypes.bfloat16)
    low = (table - high.astype(np.float64)).astype(ml_dtypes.bfloat16)
    return np.stack([high, low])


def waves(width, period):
    angle = 2.0 * np.pi / period * (np.arange(width)[:, None] * np.arange(period)[None, :] % period)
    return np.cos(angle), np.sin(angle)


def blocked_table(width, period, block):
    cosine, sine = waves(width, period)
    parts = [cosine.reshape(width, -1, 1, block), -sine.reshape(width, -1, 1, block)]
    return np.concatenate(parts, axis=2).reshape(width, 2 * period)


def split_bf16(values):
    high = values.astype(jnp.bfloat16)
    low = (values - high.astype(jnp.float32)).astype(jnp.bfloat16)
    return high, low


def dot32(left, right):
    return jnp.dot(left, right, preferred_element_type=jnp.float32)


def dot_split(stacked, high_table, low_table):
    rows = stacked.shape[0] // 2
    both = dot32(stacked, high_table)
    return both[:rows] + both[rows:] + dot32(stacked[:rows], low_table)


def swap_halves(values):
    half = LANES // 2
    parts = []
    for start in range(0, values.shape[-1], LANES):
        parts.append(pltpu.roll(values[:, start : start + LANES], half, 1))
    return jnp.concatenate(parts, axis=1) if len(parts) > 1 else parts[0]


def section_slots(map_ref, depths, sections):
    used = []
    for section in range(sections):
        found = map_ref[0] == section
        for depth in range(1, depths):
            found = jnp.logical_or(found, map_ref[depth] == section)
        used.append(found.astype(jnp.int32))
    rank, before = [], jnp.int32(0)
    for section in range(sections):
        rank.append(before)
        before = before + used[section]
    return rank, used


def slot_of_depth(map_ref, rank, depth):
    value = jnp.int32(0)
    for section, place in enumerate(rank):
        value = jnp.where(map_ref[depth] == section, place, value)
    return value


def inverse_kernel(map_ref, ret_ref, high_ref, low_ref, cos_ref, sin_ref, out_ref, split_ref):
    depths, _, rows, width = out_ref.shape
    sections = ret_ref.shape[0]
    half = depths * rows
    lanes = ret_ref.shape[2]

    @pl.when(pl.program_id(0) == 0)
    def _():
        rank, _ = section_slots(map_ref, depths, sections)
        lane = lax.broadcasted_iota(jnp.int32, (1, lanes), 1) % LANES
        sign = jnp.where(lane < LANES // 2, 1.0, -1.0)
        for depth in range(depths):
            plane = ret_ref[slot_of_depth(map_ref, rank, depth)]
            turned = (
                plane * cos_ref[pl.ds(depth, 1), :]
                - swap_halves(plane) * sin_ref[pl.ds(depth, 1), :]
            )
            crossed = swap_halves(turned) * sign
            for part, values in enumerate((turned, crossed)):
                high, low = split_bf16(values)
                split_ref[pl.ds(part * half + depth * rows, rows), :] = high
                split_ref[pl.ds((2 + part) * half + depth * rows, rows), :] = low

    product = dot_split(split_ref[...], high_ref[...], low_ref[...])
    scale = 4.0 / (lanes * lanes)
    for part in range(2):
        out_ref[:, part] = (product[part * half : (part + 1) * half] * scale).reshape(
            depths, rows, width
        )


def exchange_kernel(
    n, slots, map_ref, cos_ref, sin_ref, cur_hbm, spread_hbm, green_hbm, table_hbm, back_hbm,
    out_ref, cur, spread, split_ref, src_ref, recv, green, table, back, spectra, total, result,
    send_sem, recv_sem, send_back, recv_back, load_sem, green_sem,
):
    group = lax.axis_index("group")
    me = lax.axis_index("lat")
    rows = src_ref.shape[1]
    sections, block, period = green.shape[0], green.shape[3], green.shape[4]
    width = recv.shape[1]
    tables_in = pltpu.make_async_copy(table_hbm, table, load_sem.at[0])
    back_in = pltpu.make_async_copy(back_hbm, back, load_sem.at[1])
    green_in = pltpu.make_async_copy(green_hbm, green, green_sem)
    cur_in = pltpu.make_async_copy(cur_hbm, cur, load_sem.at[2])
    spread_in = pltpu.make_async_copy(spread_hbm, spread, load_sem.at[3])
    cur_in.start()
    spread_in.start()
    tables_in.start()

    barrier = pltpu.get_barrier_semaphore()

    def greet(step, carry):
        other = lax.rem(me + step, n)
        pl.semaphore_signal(barrier, inc=1, device_id=(group, other), device_id_type=MESH)
        return carry

    lax.fori_loop(1, n, greet, 0)
    depths, part_width = cur.shape[0], cur.shape[3]
    half = depths * rows
    cur_in.wait()
    for part in range(2):
        high, low = split_bf16(cur[:, part].reshape(half, part_width))
        split_ref[pl.ds(part * half, half), :] = high
        split_ref[pl.ds((2 + part) * half, half), :] = low
    spread_in.wait()
    pl.semaphore_wait(barrier, n - 1)

    my_rows = pl.ds(pl.multiple_of(me * rows, rows), rows)
    my_lanes = pl.ds(pl.multiple_of(me * LANES, LANES), LANES)

    def send_source(base, count, other):
        batch = pl.ds(base, count)
        lanes_there = pl.ds(pl.multiple_of(other * LANES, LANES), LANES)

        @pl.when(other != me)
        def _():
            pltpu.make_async_remote_copy(
                src_ref=src_ref.at[batch, :, lanes_there],
                dst_ref=recv.at[batch, my_rows],
                send_sem=send_sem,
                recv_sem=recv_sem.at[base // 2],
                device_id=(group, other),
                device_id_type=MESH,
            ).start()

        @pl.when(other == me)
        def _():
            pltpu.make_async_copy(
                src_ref.at[batch, :, my_lanes], recv.at[batch, my_rows], recv_sem.at[base // 2]
            ).start()

    def send_sources(base, count):
        def send(step, carry):
            send_source(base, count, lax.rem(me + n // 2 + step, n))
            return carry

        lax.fori_loop(0, n, send, 0)

    def send_results(base, count):
        batch = pl.ds(base, count)
        pltpu.make_async_copy(
            result.at[batch, my_rows], out_ref.at[batch, :, my_lanes], recv_back
        ).start()

        def send(step, carry):
            other = lax.rem(me + 1 + lax.rem(n // 2 + step, n - 1), n)
            pltpu.make_async_remote_copy(
                src_ref=result.at[batch, pl.ds(pl.multiple_of(other * rows, rows), rows)],
                dst_ref=out_ref.at[batch, :, my_lanes],
                send_sem=send_back,
                recv_sem=recv_back,
                device_id=(group, other),
                device_id_type=MESH,
            ).start()
            return carry

        lax.fori_loop(0, n - 1, send, 0)

    def batches(body, first=0):
        def pair(index, carry):
            body(index * 2, 2)
            return carry

        lax.fori_loop(first, slots // 2, pair, 0)
        if slots % 2:
            body(slots - 1, 1)

    green_in.start()
    back_in.start()
    rank, used = section_slots(map_ref, map_ref.shape[0], sections)
    place = []
    for slot in range(slots):
        found = jnp.int32(-1)
        for section in range(sections):
            here = jnp.logical_and(rank[section] == slot, used[section] == 1)
            found = jnp.where(here, section, found)
        place.append(found)

    chunk = 2 * LANES
    weights = [
        [jnp.where(map_ref[depth] == place[slot], 1.0, 0.0) for depth in range(depths)]
        for slot in range(slots)
    ]
    place = [jnp.maximum(found, 0) for found in place]

    def transform(index, carry):
        column = lax.rem(me // 2 + n // 4 + index, n // 2)
        span = pl.ds(pl.multiple_of(column * chunk, chunk), chunk)
        product = dot_split(split_ref[...], spread[0, :, span], spread[1, :, span])
        lane = lax.broadcasted_iota(jnp.int32, (1, chunk), 1) % LANES
        sign = jnp.where(lane < LANES // 2, -1.0, 1.0)
        spectrum = product[:half] + swap_halves(product[half:]) * sign
        swapped = swap_halves(spectrum)
        turned = []
        for depth in range(depths):
            at = slice(depth * rows, (depth + 1) * rows)
            turned.append(
                spectrum[at] * cos_ref[pl.ds(depth, 1), span]
                + swapped[at] * sin_ref[pl.ds(depth, 1), span]
            )
        for slot in range(slots):
            summed = turned[0] * weights[slot][0]
            for depth in range(1, depths):
                summed = summed + turned[depth] * weights[slot][depth]
            src_ref[slot, :, span] = summed
        send_source(0, 2, column * 2)
        send_source(0, 2, column * 2 + 1)
        return carry

    lax.fori_loop(0, n // 2, transform, 0)
    batches(send_sources, 1)

    def place_of(slot):
        found = place[0]
        for index in range(1, slots):
            found = jnp.where(slot == index, place[index], found)
        return found

    total[...] = jnp.zeros_like(total)
    tables_in.wait()

    def take(base, count):
        arrived = recv.at[pl.ds(base, count)]
        pltpu.make_async_copy(arrived, arrived, recv_sem.at[base // 2]).wait()
        halves = [jnp.transpose(recv[base + index]) for index in range(count)]
        stacked = jnp.concatenate(halves, axis=0) if count > 1 else halves[0]
        high, low = split_bf16(stacked)
        stacked = jnp.concatenate([high, low], axis=0)

        def columns(index, carry):
            span = pl.ds(pl.multiple_of(index * chunk, chunk), chunk)
            by_cos = dot_split(stacked, table[0, 0, :, span], table[0, 1, :, span])
            by_sin = dot_split(stacked, table[1, 0, :, span], table[1, 1, :, span])
            for slot in range(count):
                real = slice(slot * 2 * block, slot * 2 * block + block)
                imag = slice(slot * 2 * block + block, (slot + 1) * 2 * block)
                spectra[slot, 0, :, span] = by_cos[real] + by_sin[imag]
                spectra[slot, 1, :, span] = by_cos[imag] - by_sin[real]
            return carry

        lax.fori_loop(0, period // chunk, columns, 0)

        @pl.when(base == 0)
        def _():
            green_in.wait()

        froms = [place_of(base + index) for index in range(count)]

        def couple(index, carry):
            span = pl.ds(pl.multiple_of(index * 8, 8), 8)
            source = [(spectra[i, 0, span, :], spectra[i, 1, span, :]) for i in range(count)]
            for slot in range(slots):
                real = total[slot, 0, span, :]
                imag = total[slot, 1, span, :]
                for i in range(count):
                    green_real = green[place[slot], froms[i], 0, span, :]
                    green_imag = green[place[slot], froms[i], 1, span, :]
                    real = real + green_real * source[i][0] - green_imag * source[i][1]
                    imag = imag + green_real * source[i][1] + green_imag * source[i][0]
                total[slot, 0, span, :] = real
                total[slot, 1, span, :] = imag
            return carry

        lax.fori_loop(0, block // 8, couple, 0)

    batches(take)
    back_in.wait()

    def give(base, count):
        stacked = total[pl.ds(base, count)].reshape(count * 2 * block, period)
        high, low = split_bf16(stacked)
        stacked = jnp.concatenate([high, low], axis=0)

        def columns(index, carry):
            span = pl.ds(pl.multiple_of(index * chunk, chunk), chunk)
            by_cos = dot_split(stacked, back[0, 0, :, span], back[0, 1, :, span])
            by_sin = dot_split(stacked, back[1, 0, :, span], back[1, 1, :, span])
            for slot in range(count):
                real = slice(slot * 2 * block, slot * 2 * block + block)
                imag = slice(slot * 2 * block + block, (slot + 1) * 2 * block)
                plane = jnp.concatenate(
                    [by_cos[real] - by_sin[imag], by_cos[imag] + by_sin[real]], axis=0
                )
                result[base + slot, span, :] = jnp.transpose(plane)
            return carry

        lax.fori_loop(0, width // chunk, columns, 0)
        send_results(base, count)

    batches(give)
    landed = out_ref.at[pl.ds(0, slots)]
    pltpu.make_async_copy(landed, landed, recv_back).wait()
    left = src_ref.at[pl.ds(0, slots), :, pl.ds(LANES, (n - 1) * LANES)]
    pltpu.make_async_copy(left, left, send_sem).wait()
    gone = result.at[pl.ds(0, slots), pl.ds(rows, width - rows)]
    pltpu.make_async_copy(gone, gone, send_back).wait()


def most_sections(section_map, groups):
    bits = lax.reduce(
        jnp.left_shift(jnp.int32(1), section_map), np.int32(0), lax.bitwise_or, (0,)
    )
    count = lax.population_count(bits)
    most = count
    for shift in range(1, groups):
        ring = [(group, (group + shift) % groups) for group in range(groups)]
        most = jnp.maximum(most, lax.ppermute(count, "group", ring))
    return most


def per_device_kernels(n, groups, currents, green, section_map, offsets):
    depths, _, rows, width = currents.shape
    sections, _, _, block, period = green.shape
    lanes = 2 * period
    most = most_sections(section_map, groups)
    f32, bf16 = jnp.float32, jnp.bfloat16
    cosine, sine = waves(width, period)
    blocked = blocked_table(width, period, block)
    spread = jnp.asarray(split_np(blocked))
    gather = jnp.asarray(split_np(np.ascontiguousarray(blocked.T)))
    table = jnp.asarray(np.stack([split_np(cosine), split_np(sine)]))
    back = jnp.asarray(np.stack([split_np(np.ascontiguousarray(cosine.T)),
                                 split_np(np.ascontiguousarray(sine.T))]))
    lane = lax.iota(jnp.int32, lanes)
    wavenumber = lane // (2 * block) * block + lane % block
    angles = 2.0 * math.pi / period * (offsets[:, None] * wavenumber[None, :] % period).astype(f32)
    turn_cos = jnp.cos(angles)
    turn_sin = jnp.sin(angles) * jnp.where(lane % (2 * block) < block, 1.0, -1.0)
    limit = 60 * 2**20
    smem = pl.BlockSpec(memory_space=pltpu.SMEM)
    anywhere = pl.BlockSpec(memory_space=pl.ANY)
    whole = pl.BlockSpec(memory_space=pltpu.VMEM)
    column = 2 * LANES
    def exchange(slots):
        return pl.pallas_call(
            functools.partial(exchange_kernel, n, slots),
            out_shape=jax.ShapeDtypeStruct((sections, rows, lanes), f32),
            in_specs=[smem, whole, whole] + [anywhere] * 5,
            out_specs=anywhere,
            scratch_shapes=[
                pltpu.VMEM(currents.shape, f32),
                pltpu.VMEM(spread.shape, bf16),
                pltpu.VMEM((4 * depths * rows, width), bf16),
                pltpu.VMEM((slots, rows, lanes), f32),
                pltpu.VMEM((slots, width, LANES), f32),
                pltpu.VMEM(green.shape, f32),
                pltpu.VMEM(table.shape, bf16),
                pltpu.VMEM(back.shape, bf16),
                pltpu.VMEM((2, 2, block, period), f32),
                pltpu.VMEM((slots, 2, block, period), f32),
                pltpu.VMEM((slots, width, LANES), f32),
                pltpu.SemaphoreType.DMA,
                pltpu.SemaphoreType.DMA(((slots + 1) // 2,)),
                pltpu.SemaphoreType.DMA,
                pltpu.SemaphoreType.DMA,
                pltpu.SemaphoreType.DMA((4,)),
                pltpu.SemaphoreType.DMA,
            ],
            compiler_params=pltpu.CompilerParams(
                collective_id=slots, has_side_effects=True, vmem_limit_bytes=limit
            ),
        )

    fewest = sections // 2 + 1
    branches = [exchange(slots) for slots in range(fewest, sections + 1)]
    branch = jnp.clip(most - fewest, 0, sections - fewest)
    returned = lax.switch(
        branch, branches, section_map, turn_cos, turn_sin, currents, spread, green, table, back
    )
    return pl.pallas_call(
        inverse_kernel,
        grid=(width // column,),
        out_shape=jax.ShapeDtypeStruct(currents.shape, f32),
        in_specs=[
            smem,
            pl.BlockSpec((sections, rows, lanes), lambda i: (0, 0, 0)),
            pl.BlockSpec((None, lanes, column), lambda i: (0, 0, i)),
            pl.BlockSpec((None, lanes, column), lambda i: (1, 0, i)),
            pl.BlockSpec((depths, lanes), lambda i: (0, 0)),
            pl.BlockSpec((depths, lanes), lambda i: (0, 0)),
        ],
        out_specs=pl.BlockSpec((depths, 2, rows, column), lambda i: (0, 0, 0, i)),
        scratch_shapes=[pltpu.VMEM((4 * depths * rows, lanes), bf16)],
        compiler_params=pltpu.CompilerParams(vmem_limit_bytes=limit),
    )(section_map, returned, gather, gather, turn_cos, turn_sin)


def dft_table(n_in, n_out, period, sign_value):
    row_ids = lax.iota(jnp.int32, n_in)
    col_ids = lax.iota(jnp.int32, n_out)
    angles = (
        2.0 * math.pi / period * (row_ids[:, None] * col_ids[None, :] % period).astype(jnp.float32)
    )
    cosine = jnp.cos(angles)
    sine_part = sign_value * jnp.sin(angles)
    return jnp.stack(
        [jnp.stack([cosine, sine_part], axis=1), jnp.stack([-sine_part, cosine], axis=1)], axis=0
    )


def phases(offsets, period, sign_value):
    col_ids = lax.iota(jnp.int32, period)
    angles = (
        2.0 * math.pi / period * (offsets[:, None] * col_ids[None, :] % period).astype(jnp.float32)
    )
    return (jnp.cos(angles)[:, None, :], sign_value * jnp.sin(angles)[:, None, :])


def rotate(planes, cosine, sine_part):
    real_part = planes[:, 0] * cosine - planes[:, 1] * sine_part
    imag_part = planes[:, 0] * sine_part + planes[:, 1] * cosine
    return jnp.stack([real_part, imag_part], axis=1)


def per_device(currents, green, section_map, offsets):
    highest = lax.Precision.HIGHEST
    plane_width = currents.shape[3]
    padded = 2 * plane_width
    sections = green.shape[0]
    forward = dft_table(plane_width, padded, padded, -1.0)
    inverse = dft_table(padded, plane_width, padded, 1.0)
    onehot = (section_map[:, None] == lax.iota(jnp.int32, sections)[None, :]).astype(jnp.float32)
    spec_y = jnp.einsum("jcxy,cydk->jdxk", currents, forward, precision=highest)
    cos_fwd, sin_fwd = phases(offsets, padded, -1.0)
    shifted = jnp.transpose(rotate(spec_y, cos_fwd, sin_fwd), (0, 2, 1, 3))
    grouped = jnp.einsum("js,jxdk->sxdk", onehot, shifted, precision=highest)
    spectra = jnp.einsum(
        "mxcq,cxdk->mdqk",
        lax.all_to_all(grouped, "lat", split_axis=3, concat_axis=1, tiled=True),
        forward,
        precision=highest,
    )
    green_real = green[:, :, 0]
    green_imag = green[:, :, 1]
    out_real = jnp.einsum(
        "tsqk,sqk->tqk", green_real, spectra[:, 0], precision=highest
    ) - jnp.einsum("tsqk,sqk->tqk", green_imag, spectra[:, 1], precision=highest)
    out_imag = jnp.einsum(
        "tsqk,sqk->tqk", green_real, spectra[:, 1], precision=highest
    ) + jnp.einsum("tsqk,sqk->tqk", green_imag, spectra[:, 0], precision=highest)
    coupled = jnp.stack([out_real, out_imag], axis=1)
    returned = lax.all_to_all(
        jnp.einsum("mcqk,ckdx->mdxq", coupled, inverse, precision=highest),
        "lat",
        split_axis=2,
        concat_axis=3,
        tiled=True,
    )
    per_depth = jnp.einsum("js,sdxq->jdxq", onehot, returned, precision=highest)
    cos_back, sin_back = phases(offsets, padded, 1.0)
    turned = rotate(per_depth, cos_back, sin_back)
    result = jnp.einsum("jcxk,ckdy->jdxy", turned, inverse, precision=highest)
    return result * (1.0 / (padded * padded))


def solution(mesh):
    in_specs = (
        P("group", None, "lat", None),
        P("group", None, None, "lat", None),
        P("group"),
        P("group"),
    )
    out_specs = P("group", None, "lat", None)
    n, groups = mesh.shape["lat"], mesh.shape["group"]

    def either(currents, green, section_map, offsets):
        fits = 2 * green.shape[3] == LANES and green.shape[0] < 32 and currents.shape[2] % 16 == 0 and n % 4 == 0
        if fits and currents.shape[3] % (2 * LANES) == 0:
            return per_device_kernels(n, groups, currents, green, section_map, offsets)
        return per_device(currents, green, section_map, offsets)

    return jax.shard_map(
        either, mesh=mesh, in_specs=in_specs, out_specs=out_specs, check_vma=False
    )
```

```python
import functools
import math

import jax
import jax.numpy as jnp
import ml_dtypes
import numpy as np
from jax import lax
from jax.experimental import pallas as pl
from jax.experimental.pallas import tpu as pltpu
from jax.sharding import PartitionSpec as P

LANES = 128
MESH = pl.DeviceIdType.MESH


def split_np(table):
    high = table.astype(ml_dtypes.bfloat16)
    low = (table - high.astype(np.float64)).astype(ml_dtypes.bfloat16)
    return np.stack([high, low])


def waves(width, period):
    angle = 2.0 * np.pi / period * (np.arange(width)[:, None] * np.arange(period)[None, :] % period)
    return np.cos(angle), np.sin(angle)


def blocked_table(width, period, block):
    cosine, sine = waves(width, period)
    parts = [cosine.reshape(width, -1, 1, block), -sine.reshape(width, -1, 1, block)]
    return np.concatenate(parts, axis=2).reshape(width, 2 * period)


def split_bf16(values):
    high = values.astype(jnp.bfloat16)
    low = (values - high.astype(jnp.float32)).astype(jnp.bfloat16)
    return high, low


def dot32(left, right):
    return jnp.dot(left, right, preferred_element_type=jnp.float32)


def dot_split(stacked, high_table, low_table):
    rows = stacked.shape[0] // 2
    both = dot32(stacked, high_table)
    return both[:rows] + both[rows:] + dot32(stacked[:rows], low_table)


def swap_halves(values):
    half = LANES // 2
    parts = []
    for start in range(0, values.shape[-1], LANES):
        parts.append(pltpu.roll(values[:, start : start + LANES], half, 1))
    return jnp.concatenate(parts, axis=1) if len(parts) > 1 else parts[0]


def section_slots(map_ref, depths, sections):
    used = []
    for section in range(sections):
        found = map_ref[0] == section
        for depth in range(1, depths):
            found = jnp.logical_or(found, map_ref[depth] == section)
        used.append(found.astype(jnp.int32))
    rank, before = [], jnp.int32(0)
    for section in range(sections):
        rank.append(before)
        before = before + used[section]
    return rank, used


def slot_of_depth(map_ref, rank, depth):
    value = jnp.int32(0)
    for section, place in enumerate(rank):
        value = jnp.where(map_ref[depth] == section, place, value)
    return value


def inverse_kernel(map_ref, ret_ref, high_ref, low_ref, cos_ref, sin_ref, out_ref, split_ref):
    depths, _, rows, width = out_ref.shape
    sections = ret_ref.shape[0]
    half = depths * rows
    lanes = ret_ref.shape[2]

    @pl.when(pl.program_id(0) == 0)
    def _():
        rank, _ = section_slots(map_ref, depths, sections)
        lane = lax.broadcasted_iota(jnp.int32, (1, lanes), 1) % LANES
        sign = jnp.where(lane < LANES // 2, 1.0, -1.0)
        for depth in range(depths):
            plane = ret_ref[slot_of_depth(map_ref, rank, depth)]
            turned = (
                plane * cos_ref[pl.ds(depth, 1), :]
                - swap_halves(plane) * sin_ref[pl.ds(depth, 1), :]
            )
            crossed = swap_halves(turned) * sign
            for part, values in enumerate((turned, crossed)):
                high, low = split_bf16(values)
                split_ref[pl.ds(part * half + depth * rows, rows), :] = high
                split_ref[pl.ds((2 + part) * half + depth * rows, rows), :] = low

    product = dot_split(split_ref[...], high_ref[...], low_ref[...])
    scale = 4.0 / (lanes * lanes)
    for part in range(2):
        out_ref[:, part] = (product[part * half : (part + 1) * half] * scale).reshape(
            depths, rows, width
        )


def exchange_kernel(
    n, slots, map_ref, cos_ref, sin_ref, cur_hbm, spread_hbm, green_hbm, table_hbm, back_hbm,
    out_ref, cur, spread, split_ref, src_ref, recv, green, table, back, spectra, total, result,
    send_sem, recv_sem, send_back, recv_back, load_sem, green_sem,
):
    group = lax.axis_index("group")
    me = lax.axis_index("lat")
    rows = src_ref.shape[1]
    sections, block, period = green.shape[0], green.shape[3], green.shape[4]
    width = recv.shape[1]
    tables_in = pltpu.make_async_copy(table_hbm, table, load_sem.at[0])
    back_in = pltpu.make_async_copy(back_hbm, back, load_sem.at[1])
    green_in = pltpu.make_async_copy(green_hbm, green, green_sem)
    cur_in = pltpu.make_async_copy(cur_hbm, cur, load_sem.at[2])
    spread_in = pltpu.make_async_copy(spread_hbm, spread, load_sem.at[3])
    cur_in.start()
    spread_in.start()
    tables_in.start()

    barrier = pltpu.get_barrier_semaphore()

    def greet(step, carry):
        other = lax.rem(me + step, n)
        pl.semaphore_signal(barrier, inc=1, device_id=(group, other), device_id_type=MESH)
        return carry

    lax.fori_loop(1, n, greet, 0)
    depths, part_width = cur.shape[0], cur.shape[3]
    half = depths * rows
    cur_in.wait()
    for part in range(2):
        high, low = split_bf16(cur[:, part].reshape(half, part_width))
        split_ref[pl.ds(part * half, half), :] = high
        split_ref[pl.ds((2 + part) * half, half), :] = low
    spread_in.wait()
    pl.semaphore_wait(barrier, n - 1)

    my_rows = pl.ds(pl.multiple_of(me * rows, rows), rows)
    my_lanes = pl.ds(pl.multiple_of(me * LANES, LANES), LANES)

    def send_source(base, count, other):
        batch = pl.ds(base, count)
        lanes_there = pl.ds(pl.multiple_of(other * LANES, LANES), LANES)

        @pl.when(other != me)
        def _():
            pltpu.make_async_remote_copy(
                src_ref=src_ref.at[batch, :, lanes_there],
                dst_ref=recv.at[batch, my_rows],
                send_sem=send_sem,
                recv_sem=recv_sem.at[base // 2],
                device_id=(group, other),
                device_id_type=MESH,
            ).start()

        @pl.when(other == me)
        def _():
            pltpu.make_async_copy(
                src_ref.at[batch, :, my_lanes], recv.at[batch, my_rows], recv_sem.at[base // 2]
            ).start()

    def send_sources(base, count):
        def send(step, carry):
            send_source(base, count, lax.rem(me + n // 2 + step, n))
            return carry

        lax.fori_loop(0, n, send, 0)

    def send_result(base, count, other):
        batch = pl.ds(base, count)
        rows_there = pl.ds(pl.multiple_of(other * rows, rows), rows)

        @pl.when(other != me)
        def _():
            pltpu.make_async_remote_copy(
                src_ref=result.at[batch, rows_there],
                dst_ref=out_ref.at[batch, :, my_lanes],
                send_sem=send_back,
                recv_sem=recv_back,
                device_id=(group, other),
                device_id_type=MESH,
            ).start()

        @pl.when(other == me)
        def _():
            pltpu.make_async_copy(
                result.at[batch, my_rows], out_ref.at[batch, :, my_lanes], recv_back
            ).start()

    def batches(body, first=0):
        def pair(index, carry):
            body(index * 2, 2)
            return carry

        lax.fori_loop(first, slots // 2, pair, 0)
        if slots % 2:
            body(slots - 1, 1)

    rank, used = section_slots(map_ref, map_ref.shape[0], sections)
    place = []
    for slot in range(slots):
        found = jnp.int32(-1)
        for section in range(sections):
            here = jnp.logical_and(rank[section] == slot, used[section] == 1)
            found = jnp.where(here, section, found)
        place.append(found)

    chunk = 2 * LANES
    weights = [
        [jnp.where(map_ref[depth] == place[slot], 1.0, 0.0) for depth in range(depths)]
        for slot in range(slots)
    ]
    place = [jnp.maximum(found, 0) for found in place]

    def transform(index, carry):
        column = lax.rem(me // 2 + n // 4 + index, n // 2)
        span = pl.ds(pl.multiple_of(column * chunk, chunk), chunk)
        product = dot_split(split_ref[...], spread[0, :, span], spread[1, :, span])
        lane = lax.broadcasted_iota(jnp.int32, (1, chunk), 1) % LANES
        sign = jnp.where(lane < LANES // 2, -1.0, 1.0)
        spectrum = product[:half] + swap_halves(product[half:]) * sign
        swapped = swap_halves(spectrum)
        turned = []
        for depth in range(depths):
            at = slice(depth * rows, (depth + 1) * rows)
            turned.append(
                spectrum[at] * cos_ref[pl.ds(depth, 1), span]
                + swapped[at] * sin_ref[pl.ds(depth, 1), span]
            )
        for slot in range(slots):
            summed = turned[0] * weights[slot][0]
            for depth in range(1, depths):
                summed = summed + turned[depth] * weights[slot][depth]
            src_ref[slot, :, span] = summed
        send_source(0, 2, column * 2)
        send_source(0, 2, column * 2 + 1)
        return carry

    lax.fori_loop(0, n // 2, transform, 0)
    batches(send_sources, 1)
    green_in.start()
    back_in.start()

    def place_of(slot):
        found = place[0]
        for index in range(1, slots):
            found = jnp.where(slot == index, place[index], found)
        return found

    total[...] = jnp.zeros_like(total)
    tables_in.wait()

    def take(base, count):
        arrived = recv.at[pl.ds(base, count)]
        pltpu.make_async_copy(arrived, arrived, recv_sem.at[base // 2]).wait()
        halves = [jnp.transpose(recv[base + index]) for index in range(count)]
        stacked = jnp.concatenate(halves, axis=0) if count > 1 else halves[0]
        high, low = split_bf16(stacked)
        stacked = jnp.concatenate([high, low], axis=0)

        def columns(index, carry):
            span = pl.ds(pl.multiple_of(index * chunk, chunk), chunk)
            by_cos = dot_split(stacked, table[0, 0, :, span], table[0, 1, :, span])
            by_sin = dot_split(stacked, table[1, 0, :, span], table[1, 1, :, span])
            for slot in range(count):
                real = slice(slot * 2 * block, slot * 2 * block + block)
                imag = slice(slot * 2 * block + block, (slot + 1) * 2 * block)
                spectra[slot, 0, :, span] = by_cos[real] + by_sin[imag]
                spectra[slot, 1, :, span] = by_cos[imag] - by_sin[real]
            return carry

        lax.fori_loop(0, period // chunk, columns, 0)

        @pl.when(base == 0)
        def _():
            green_in.wait()

        froms = [place_of(base + index) for index in range(count)]

        def couple(index, carry):
            span = pl.ds(pl.multiple_of(index * 8, 8), 8)
            source = [(spectra[i, 0, span, :], spectra[i, 1, span, :]) for i in range(count)]
            for slot in range(slots):
                real = total[slot, 0, span, :]
                imag = total[slot, 1, span, :]
                for i in range(count):
                    green_real = green[place[slot], froms[i], 0, span, :]
                    green_imag = green[place[slot], froms[i], 1, span, :]
                    real = real + green_real * source[i][0] - green_imag * source[i][1]
                    imag = imag + green_real * source[i][1] + green_imag * source[i][0]
                total[slot, 0, span, :] = real
                total[slot, 1, span, :] = imag
            return carry

        lax.fori_loop(0, block // 8, couple, 0)

    batches(take)
    back_in.wait()

    def give(base, count):
        stacked = total[pl.ds(base, count)].reshape(count * 2 * block, period)
        high, low = split_bf16(stacked)
        stacked = jnp.concatenate([high, low], axis=0)

        def columns(index, carry):
            column = lax.rem(me * rows // chunk + width // chunk // 2 + index, width // chunk)
            span = pl.ds(pl.multiple_of(column * chunk, chunk), chunk)
            by_cos = dot_split(stacked, back[0, 0, :, span], back[0, 1, :, span])
            by_sin = dot_split(stacked, back[1, 0, :, span], back[1, 1, :, span])
            for slot in range(count):
                real = slice(slot * 2 * block, slot * 2 * block + block)
                imag = slice(slot * 2 * block + block, (slot + 1) * 2 * block)
                plane = jnp.concatenate(
                    [by_cos[real] - by_sin[imag], by_cos[imag] + by_sin[real]], axis=0
                )
                result[base + slot, span, :] = jnp.transpose(plane)
            first = column * (chunk // rows)

            def send(step, inner):
                send_result(base, count, first + step)
                return inner

            lax.fori_loop(0, chunk // rows, send, 0)
            return carry

        lax.fori_loop(0, width // chunk, columns, 0)

    batches(give)
    landed = out_ref.at[pl.ds(0, slots)]
    pltpu.make_async_copy(landed, landed, recv_back).wait()
    left = src_ref.at[pl.ds(0, slots), :, pl.ds(LANES, (n - 1) * LANES)]
    pltpu.make_async_copy(left, left, send_sem).wait()
    gone = result.at[pl.ds(0, slots), pl.ds(rows, width - rows)]
    pltpu.make_async_copy(gone, gone, send_back).wait()


def most_sections(section_map, groups):
    bits = lax.reduce(
        jnp.left_shift(jnp.int32(1), section_map), np.int32(0), lax.bitwise_or, (0,)
    )
    count = lax.population_count(bits)
    most = count
    for shift in range(1, groups):
        ring = [(group, (group + shift) % groups) for group in range(groups)]
        most = jnp.maximum(most, lax.ppermute(count, "group", ring))
    return most


def per_device_kernels(n, groups, currents, green, section_map, offsets):
    depths, _, rows, width = currents.shape
    sections, _, _, block, period = green.shape
    lanes = 2 * period
    most = most_sections(section_map, groups)
    f32, bf16 = jnp.float32, jnp.bfloat16
    cosine, sine = waves(width, period)
    blocked = blocked_table(width, period, block)
    spread = jnp.asarray(split_np(blocked))
    gather = jnp.asarray(split_np(np.ascontiguousarray(blocked.T)))
    table = jnp.asarray(np.stack([split_np(cosine), split_np(sine)]))
    back = jnp.asarray(np.stack([split_np(np.ascontiguousarray(cosine.T)),
                                 split_np(np.ascontiguousarray(sine.T))]))
    lane = lax.iota(jnp.int32, lanes)
    wavenumber = lane // (2 * block) * block + lane % block
    angles = 2.0 * math.pi / period * (offsets[:, None] * wavenumber[None, :] % period).astype(f32)
    turn_cos = jnp.cos(angles)
    turn_sin = jnp.sin(angles) * jnp.where(lane % (2 * block) < block, 1.0, -1.0)
    limit = 60 * 2**20
    smem = pl.BlockSpec(memory_space=pltpu.SMEM)
    anywhere = pl.BlockSpec(memory_space=pl.ANY)
    whole = pl.BlockSpec(memory_space=pltpu.VMEM)
    column = 2 * LANES
    def exchange(slots):
        return pl.pallas_call(
            functools.partial(exchange_kernel, n, slots),
            out_shape=jax.ShapeDtypeStruct((sections, rows, lanes), f32),
            in_specs=[smem, whole, whole] + [anywhere] * 5,
            out_specs=anywhere,
            scratch_shapes=[
                pltpu.VMEM(currents.shape, f32),
                pltpu.VMEM(spread.shape, bf16),
                pltpu.VMEM((4 * depths * rows, width), bf16),
                pltpu.VMEM((slots, rows, lanes), f32),
                pltpu.VMEM((slots, width, LANES), f32),
                pltpu.VMEM(green.shape, f32),
                pltpu.VMEM(table.shape, bf16),
                pltpu.VMEM(back.shape, bf16),
                pltpu.VMEM((2, 2, block, period), f32),
                pltpu.VMEM((slots, 2, block, period), f32),
                pltpu.VMEM((slots, width, LANES), f32),
                pltpu.SemaphoreType.DMA,
                pltpu.SemaphoreType.DMA(((slots + 1) // 2,)),
                pltpu.SemaphoreType.DMA,
                pltpu.SemaphoreType.DMA,
                pltpu.SemaphoreType.DMA((4,)),
                pltpu.SemaphoreType.DMA,
            ],
            compiler_params=pltpu.CompilerParams(
                collective_id=slots, has_side_effects=True, vmem_limit_bytes=limit
            ),
        )

    fewest = sections // 2 + 1
    branches = [exchange(slots) for slots in range(fewest, sections + 1)]
    branch = jnp.clip(most - fewest, 0, sections - fewest)
    returned = lax.switch(
        branch, branches, section_map, turn_cos, turn_sin, currents, spread, green, table, back
    )
    return pl.pallas_call(
        inverse_kernel,
        grid=(width // column,),
        out_shape=jax.ShapeDtypeStruct(currents.shape, f32),
        in_specs=[
            smem,
            pl.BlockSpec((sections, rows, lanes), lambda i: (0, 0, 0)),
            pl.BlockSpec((None, lanes, column), lambda i: (0, 0, i)),
            pl.BlockSpec((None, lanes, column), lambda i: (1, 0, i)),
            pl.BlockSpec((depths, lanes), lambda i: (0, 0)),
            pl.BlockSpec((depths, lanes), lambda i: (0, 0)),
        ],
        out_specs=pl.BlockSpec((depths, 2, rows, column), lambda i: (0, 0, 0, i)),
        scratch_shapes=[pltpu.VMEM((4 * depths * rows, lanes), bf16)],
        compiler_params=pltpu.CompilerParams(vmem_limit_bytes=limit),
    )(section_map, returned, gather, gather, turn_cos, turn_sin)


def dft_table(n_in, n_out, period, sign_value):
    row_ids = lax.iota(jnp.int32, n_in)
    col_ids = lax.iota(jnp.int32, n_out)
    angles = (
        2.0 * math.pi / period * (row_ids[:, None] * col_ids[None, :] % period).astype(jnp.float32)
    )
    cosine = jnp.cos(angles)
    sine_part = sign_value * jnp.sin(angles)
    return jnp.stack(
        [jnp.stack([cosine, sine_part], axis=1), jnp.stack([-sine_part, cosine], axis=1)], axis=0
    )


def phases(offsets, period, sign_value):
    col_ids = lax.iota(jnp.int32, period)
    angles = (
        2.0 * math.pi / period * (offsets[:, None] * col_ids[None, :] % period).astype(jnp.float32)
    )
    return (jnp.cos(angles)[:, None, :], sign_value * jnp.sin(angles)[:, None, :])


def rotate(planes, cosine, sine_part):
    real_part = planes[:, 0] * cosine - planes[:, 1] * sine_part
    imag_part = planes[:, 0] * sine_part + planes[:, 1] * cosine
    return jnp.stack([real_part, imag_part], axis=1)


def per_device(currents, green, section_map, offsets):
    highest = lax.Precision.HIGHEST
    plane_width = currents.shape[3]
    padded = 2 * plane_width
    sections = green.shape[0]
    forward = dft_table(plane_width, padded, padded, -1.0)
    inverse = dft_table(padded, plane_width, padded, 1.0)
    onehot = (section_map[:, None] == lax.iota(jnp.int32, sections)[None, :]).astype(jnp.float32)
    spec_y = jnp.einsum("jcxy,cydk->jdxk", currents, forward, precision=highest)
    cos_fwd, sin_fwd = phases(offsets, padded, -1.0)
    shifted = jnp.transpose(rotate(spec_y, cos_fwd, sin_fwd), (0, 2, 1, 3))
    grouped = jnp.einsum("js,jxdk->sxdk", onehot, shifted, precision=highest)
    spectra = jnp.einsum(
        "mxcq,cxdk->mdqk",
        lax.all_to_all(grouped, "lat", split_axis=3, concat_axis=1, tiled=True),
        forward,
        precision=highest,
    )
    green_real = green[:, :, 0]
    green_imag = green[:, :, 1]
    out_real = jnp.einsum(
        "tsqk,sqk->tqk", green_real, spectra[:, 0], precision=highest
    ) - jnp.einsum("tsqk,sqk->tqk", green_imag, spectra[:, 1], precision=highest)
    out_imag = jnp.einsum(
        "tsqk,sqk->tqk", green_real, spectra[:, 1], precision=highest
    ) + jnp.einsum("tsqk,sqk->tqk", green_imag, spectra[:, 0], precision=highest)
    coupled = jnp.stack([out_real, out_imag], axis=1)
    returned = lax.all_to_all(
        jnp.einsum("mcqk,ckdx->mdxq", coupled, inverse, precision=highest),
        "lat",
        split_axis=2,
        concat_axis=3,
        tiled=True,
    )
    per_depth = jnp.einsum("js,sdxq->jdxq", onehot, returned, precision=highest)
    cos_back, sin_back = phases(offsets, padded, 1.0)
    turned = rotate(per_depth, cos_back, sin_back)
    result = jnp.einsum("jcxk,ckdy->jdxy", turned, inverse, precision=highest)
    return result * (1.0 / (padded * padded))


def solution(mesh):
    in_specs = (
        P("group", None, "lat", None),
        P("group", None, None, "lat", None),
        P("group"),
        P("group"),
    )
    out_specs = P("group", None, "lat", None)
    n, groups = mesh.shape["lat"], mesh.shape["group"]

    def either(currents, green, section_map, offsets):
        fits = 2 * green.shape[3] == LANES and green.shape[0] < 32
        fits = fits and currents.shape[2] in (16, 32, 64) and n % 4 == 0
        if fits and currents.shape[3] % (2 * LANES) == 0:
            return per_device_kernels(n, groups, currents, green, section_map, offsets)
        return per_device(currents, green, section_map, offsets)

    return jax.shard_map(
        either, mesh=mesh, in_specs=in_specs, out_specs=out_specs, check_vma=False
    )
```
